256 devices in a mesh: rep: 32 (over z, y), fsdp: 8 (over x, core).
Axes of the slice: x: 4, y: 4, z: 8, core: 2. Of those that a mesh axis runs over, the one named last changes fastest.
Arguments:
- tokens: bfloat16 [131072, 4096], P(('rep', 'fsdp')), may hold values from -6 to 6
- cotangent: bfloat16 [131072, 512], P(('rep', 'fsdp')), may hold values from -6 to 6
- inner_params: bfloat16 [32, 4096, 512], P('rep', 'fsdp'), may hold values from -6 to 6
- first_moment: float32 [32, 4096, 512], P('rep', 'fsdp'), may hold values from -2 to 2
- second_moment: float32 [32, 4096, 512], P('rep', 'fsdp'), may hold values from 0.01 to 1
- anchor: float32 [4096, 512], P('fsdp'), may hold values from -6 to 6
- feedback: float32 [32, 4096, 512], P('rep', 'fsdp'), may hold values from -4 to 4
- momentum: float32 [4096, 512], P('fsdp'), may hold values from -4 to 4
- sel_blocks: int32 [32, 8, 256], P('rep', 'fsdp'), may hold values from 0 to 1023, as said below
- sel_count: int32 [32, 8], P('rep', 'fsdp'), may hold values from 64 to 256
Outputs:
- key_out: bfloat16 [131072, 512], P(('rep', 'fsdp'))
- anchor_new: float32 [4096, 512], P('fsdp')
- feedback_new: float32 [32, 4096, 512], P('rep', 'fsdp')
- momentum_new: float32 [4096, 512], P('fsdp')
The draws below stay inside these ranges and needn't reach their ends.
Inputs may be any that keep to these rules, and one draw needn't show every extreme that they name: `sel_blocks`: the first sel_count[r, f] entries of list (r, f) are distinct blocks of the shard's 1024; the entries past them are other blocks of the shard, not selected. Owner o's range is blocks o * 32 up to (o + 1) * 32; at most 16 selected blocks of one list lie in one owner's range. For each fsdp index, one owner's range holds exactly 16 selected blocks of every list.
All inputs are finite; a program needn't handle non-finite values.
Results may differ from the reference program's by a relative error of at most 0.004.
Values may be sent and summed in bfloat16 or wider, within the bound.
A program may use at most 128 MiB of HBM per device.

```python
import math
import jax
import jax.numpy as jnp
from jax import lax

D = 4096
BLK = 256
TOK_DEV = 512
C = 512
NB = 1024
KSEL = 256
CAP = 16
TOKENS = 131072
N_REP = 32
N_FSDP = 8


def choose_lists(key):
    list_count = N_REP * N_FSDP
    key_count, key_full, key_hot, key_score = jax.random.split(key, 4)
    lower = KSEL // 4
    cubes = jax.random.randint(key_count, (list_count,), 0, 64)
    amount = lower + (KSEL - lower) * (cubes * cubes * cubes) // (63 * 63 * 63)
    full_at = jax.random.randint(key_full, (), 0, list_count)
    positions = jnp.arange(list_count)
    amount = jnp.where(positions == full_at, KSEL, amount)
    amount = jnp.where(positions == (full_at + 1) % list_count, lower, amount)
    hot_owner = jax.random.randint(key_hot, (N_FSDP,), 0, N_REP)
    hot_per_list = jnp.broadcast_to(hot_owner[None, :], (N_REP, N_FSDP)).reshape(list_count)
    random_part = jax.random.randint(key_score, (list_count, NB), 0, 2 ** 29 // NB)
    scores = random_part * NB + jnp.arange(NB)[None, :]
    grouped = scores.reshape(list_count, N_REP, NB // N_REP)
    ordering = jnp.argsort(-grouped, axis=-1)
    ranking = jnp.argsort(ordering, axis=-1)
    eligible = (ranking < CAP).reshape(list_count, NB).astype(jnp.int32)
    owner_index = jnp.arange(NB) // (NB // N_REP)
    hot_block = (owner_index[None, :] == hot_per_list[:, None]).astype(jnp.int32)
    priority = eligible * 2 ** 30 + hot_block * 2 ** 29 + scores
    chosen = jnp.argsort(-priority, axis=-1)[:, :KSEL].astype(jnp.int32)
    return (chosen.reshape(N_REP, N_FSDP, KSEL), amount.reshape(N_REP, N_FSDP).astype(jnp.int32))


def draw_sel_blocks(key, part):
    chosen, amount = choose_lists(key)
    return chosen


def draw_sel_count(key, part):
    chosen, amount = choose_lists(key)
    return amount


def shard_levels(own_key, dims, cuts, low, top_value):
    factor_of = 1.0
    for position, shards_of in cuts:
        heights = jax.random.uniform(jax.random.fold_in(jax.random.fold_in(own_key, 6), position), (shards_of,), jnp.float32, low / len(cuts), top_value / len(cuts))
        factor_of = factor_of * jnp.repeat(jnp.exp(heights), dims[position] // shards_of).reshape((-1,) + (1,) * (len(dims) - 1 - position))
    return factor_of


def noise(own_key, dims, scale, reach, cuts=(), held_as=jnp.bfloat16):
    result = jax.random.normal(own_key, dims, jnp.float32) * scale
    if len(cuts) > 0:
        result = shard_levels(own_key, dims, cuts, -0.22, 0.18) * result
    return jnp.clip(result, min=-reach, max=reach).astype(held_as)


def setup_inputs(seed: int = 0) -> dict:
    key_of = jax.random.split(jax.random.key(seed), 11)
    tokens = noise(key_of[0], (TOKENS, D), 1.0, 6.0, ((0, 256),))
    cotangent = noise(key_of[1], (TOKENS, C), 1.0, 6.0, ((0, 256),))
    inner_params = noise(key_of[2], (N_REP, D, C), 1.0, 6.0, ((0, 32), (1, 8)))
    first_moment = noise(key_of[3], (N_REP, D, C), 0.3, 2.0, ((0, 32), (1, 8)), jnp.float32)
    second_moment = jnp.clip(jnp.exp(math.log(1.0) - 4.6051702 * jax.random.uniform(key_of[4], (N_REP, D, C), jnp.float32) ** shard_levels(key_of[4], (N_REP, D, C), ((0, 32), (1, 8)), -0.2, 0.2)), 0.01, 1.0)
    anchor = noise(key_of[5], (D, C), 1.0, 6.0, ((0, 8),), jnp.float32)
    feedback = noise(key_of[6], (N_REP, D, C), 0.5, 4.0, ((0, 32), (1, 8)), jnp.float32)
    momentum = noise(key_of[7], (D, C), 0.5, 4.0, ((0, 8),), jnp.float32)
    sel_blocks = draw_sel_blocks(jax.random.fold_in(key_of[10], 71), 0)
    sel_count = draw_sel_count(jax.random.fold_in(key_of[10], 71), 0)
    return {"tokens": tokens, "cotangent": cotangent, "inner_params": inner_params, "first_moment": first_moment, "second_moment": second_moment, "anchor": anchor, "feedback": feedback, "momentum": momentum, "sel_blocks": sel_blocks, "sel_count": sel_count}


beta_first = 0.9
beta_second = 0.95
epsilon = 1e-08
decay_rate = 0.1
inner_rate = 1.0
outer_rate = 0.7
outer_momentum = 0.9

def shard_mask(blocks, amount):
    usable = (jnp.arange(KSEL, dtype=jnp.int32)[None, :] < amount[:, None]).astype(jnp.float32)
    shards = jnp.arange(N_FSDP, dtype=jnp.int32)[:, None] * jnp.ones((1, KSEL), jnp.int32)
    marked = jnp.zeros((N_FSDP, NB), jnp.float32).at[shards, blocks].max(usable)
    marked = jnp.broadcast_to(marked.reshape(N_FSDP, D // N_FSDP, C // BLK, 1), (N_FSDP, D // N_FSDP, C // BLK, BLK))
    return marked.reshape(D, C)

def reference(tokens, cotangent, inner_params, first_moment, second_moment, anchor, feedback, momentum, sel_blocks, sel_count):
    inverse = 1.0 / math.sqrt(D)
    token_groups = tokens.reshape(N_REP, N_FSDP, TOK_DEV, D)
    cotangent_groups = cotangent.reshape(N_REP, N_FSDP, TOK_DEV, C)

    def forward(operands):
        inputs, weights = operands
        product = jnp.dot(inputs.reshape(N_FSDP * TOK_DEV, D), weights, preferred_element_type=jnp.float32)
        return (product * inverse).astype(jnp.bfloat16)
    key_out = lax.map(forward, (token_groups, inner_params)).reshape(TOKENS, C)

    def partial_term(operands):
        inputs, upstream = operands
        partial_value = lax.dot_general(inputs, upstream, (((0,), (0,)), ((), ())), preferred_element_type=jnp.float32) * inverse
        return lax.optimization_barrier(partial_value.astype(jnp.bfloat16)).astype(jnp.float32)

    def replica_step(summed, sliced):
        inputs, upstream, weights, moment_one, moment_two, residue, blocks, amount = sliced
        gradient = lax.optimization_barrier(jnp.sum(lax.map(partial_term, (inputs, upstream)), axis=0))
        first_new = beta_first * moment_one + (1.0 - beta_first) * gradient
        second_new = beta_second * moment_two + (1.0 - beta_second) * gradient * gradient
        master = weights.astype(jnp.float32)
        stepped = master - inner_rate * (first_new / (jnp.sqrt(second_new) + epsilon) + decay_rate * master)
        combined = residue + (anchor - stepped)
        marked = shard_mask(blocks, amount)
        outgoing = jnp.where(marked > 0.0, combined, 0.0)
        kept = jnp.where(marked > 0.0, 0.0, combined)
        return (summed + outgoing, kept)
    summed, feedback_new = lax.scan(replica_step, jnp.zeros((D, C), jnp.float32), (token_groups, cotangent_groups, inner_params, first_moment, second_moment, feedback, sel_blocks, sel_count))
    average = summed / N_REP
    momentum_new = outer_momentum * momentum + average
    anchor_new = anchor - outer_rate * (average + outer_momentum * momentum_new)
    return (key_out, anchor_new, feedback_new, momentum_new)
```

```python
import math

import jax
import jax.numpy as jnp
from jax import lax
from jax.experimental import pallas as pl
from jax.experimental.pallas import tpu as pltpu
from jax.sharding import PartitionSpec as P

D = 4096
BLK = 256
COLS = 512
ROWS = 512
TOK = 512
KSEL = 256
NX = 4
NY = 4
NZ = 8
NP = 2
W = COLS // NP
HALF = W // 2
YR = ROWS // NY
ZR = YR // NZ

beta_first = 0.9
beta_second = 0.95
epsilon = 1e-08
decay_rate = 0.1
inner_rate = 1.0
outer_rate = 0.7
outer_momentum = 0.9

MESH = pl.DeviceIdType.MESH
F32 = jnp.float32
BF16 = jnp.bfloat16

ORDER = (2, 1, 3, 0)


def kernel(
    tok_hbm, cot_hbm, par_hbm, first_hbm, second_hbm, anchor_hbm, feed_hbm, mom_hbm, sel_hbm, cnt_hbm,
    key_hbm, anchor_out, feed_out, mom_out,
    tok, cot, cot_t, wts, first, second, anchor, feed, mom, sel, cnt,
    part, sib_in, msg, fin, grad_t, mark, outg, ybuf, zsrc, zbuf, avg,
    acc, key_v, anchor_v, feed_v, mom_v,
    load_sem, store_sem,
    sib_s, sib_r, x_s, x_r, ag_s, ag_r, rel_s, rel_r,
    y_s, y_r, z_s, z_r, gz_s, gz_r, gy_s, gy_r,
):
    rep = lax.axis_index("rep")
    fs = lax.axis_index("fsdp")
    core = lax.rem(fs, 2)
    x = fs // 2
    y = lax.rem(rep, NY)
    z = rep // NY

    def on_x(k):
        return (rep, lax.rem(x + k, NX) * 2 + core)

    def on_y(k):
        return (z * NY + lax.rem(y + k, NY), fs)

    def on_z(k):
        return (lax.rem(z + k, NZ) * NY + y, fs)

    sib = (rep, x * 2 + 1 - core)

    def remote(src, dst, send, recv, dev):
        return pltpu.make_async_remote_copy(
            src_ref=src, dst_ref=dst, send_sem=send, recv_sem=recv, device_id=dev, device_id_type=MESH
        )

    loads = []

    def load(src, dst):
        c = pltpu.make_async_copy(src, dst, load_sem.at[len(loads)])
        loads.append(c)
        c.start()
        return c

    l_cot = load(cot_hbm, cot)
    l_w = load(par_hbm.at[0], wts.at[7])
    l_tok = []
    for i in range(8):
        chip = lax.rem(x + ORDER[i // 2], NX)
        shard = chip * 2 + (1 - core if i % 2 == 0 else core)
        l_tok.append(load(tok_hbm.at[:, pl.ds(pl.multiple_of(shard * ROWS, ROWS), ROWS)], tok.at[i]))
    l_sel = load(sel_hbm, sel)
    l_cnt = load(cnt_hbm, cnt)
    l_state = [
        load(first_hbm.at[0], first),
        load(second_hbm.at[0], second),
        load(anchor_hbm, anchor),
        load(feed_hbm.at[0], feed),
        load(mom_hbm, mom),
    ]

    barrier = pltpu.get_barrier_semaphore()
    peers = [sib, on_x(1), on_x(3)] + [on_y(k) for k in range(1, NY)] + [on_z(k) for k in range(1, NZ)]
    for dev in peers:
        pl.semaphore_signal(barrier, inc=1, device_id=dev, device_id_type=MESH)

    l_cot.wait()
    cot_t[...] = jnp.transpose(cot[...], (1, 0))
    l_w.wait()
    pl.semaphore_wait(barrier, len(peers))

    def ag(n, src_slot, rows, dst_slot, k):
        c = remote(
            wts.at[src_slot, pl.ds(rows, 256)], wts.at[dst_slot, pl.ds(rows, 256)], ag_s.at[n], ag_r.at[n], on_x(k)
        )
        c.start()
        return c

    ag_plus_a = ag(0, 7, 0, 5, 1)
    ag_minus_b = ag(1, 7, 256, 3, 3)

    def products(h):
        def body(i, _):
            p = lax.dot_general(
                cot_t[h * W : (h + 1) * W, :], tok[i], (((1,), (0,)), ((), ())), preferred_element_type=F32
            )
            part[h, i] = (p * (1.0 / math.sqrt(D))).astype(BF16)
            return 0

        copies = []
        for i in range(8):
            if h == 0:
                l_tok[i].wait()
            body(i, 0)
            if i % 2 == 0:
                c = remote(part.at[h, i], sib_in.at[h, i // 2], sib_s.at[h, i // 2], sib_r.at[h, i // 2], sib)
                c.start()
                copies.append(c)
        return copies

    def x_send(h, n, src, dst, k):
        c = remote(src, dst, x_s.at[h, n], x_r.at[h, n], on_x(k))
        c.start()
        return c

    def pair_sum(h, i, rows):
        return part[h, 2 * i + 1, rows : rows + HALF, :].astype(F32) + sib_in[h, i, rows : rows + HALF, :].astype(F32)

    A, B = 0, HALF

    def x_first(h, sib_c):
        sib_c[0].wait_recv()
        msg[h, 0] = pair_sum(h, 0, A).astype(BF16)
        c0 = x_send(h, 0, msg.at[h, 0], fin.at[h, 0, pl.ds(A, HALF)], 1)
        msg[h, 1] = pair_sum(h, 0, B).astype(BF16)
        c1 = x_send(h, 1, msg.at[h, 1], fin.at[h, 0, pl.ds(B, HALF)], 3)
        sib_c[1].wait_recv()
        msg[h, 2] = pair_sum(h, 1, B).astype(BF16)
        c2 = x_send(h, 2, msg.at[h, 2], fin.at[h, 1, pl.ds(B, HALF)], 1)
        sib_c[2].wait_recv()
        msg[h, 3] = pair_sum(h, 2, A).astype(BF16)
        c3 = x_send(h, 3, msg.at[h, 3], fin.at[h, 2, pl.ds(A, HALF)], 3)
        return [c0, c1, c2, c3]

    def x_second(h, c):
        c[0].wait_recv()
        msg[h, 4] = (pair_sum(h, 1, A) + fin[h, 0, A : A + HALF, :].astype(F32)).astype(BF16)
        c4 = x_send(h, 4, msg.at[h, 4], fin.at[h, 1, pl.ds(A, HALF)], 1)
        c[1].wait_recv()
        msg[h, 5] = (pair_sum(h, 2, B) + fin[h, 0, B : B + HALF, :].astype(F32)).astype(BF16)
        c5 = x_send(h, 5, msg.at[h, 5], fin.at[h, 2, pl.ds(B, HALF)], 3)
        return c + [c4, c5]

    def marks():
        l_sel.wait()
        l_cnt.wait()
        place = lax.broadcasted_iota(jnp.int32, (1, KSEL), 1)
        names = jnp.where(place < cnt[...], sel[...], -1)
        ones = jnp.ones((KSEL, W), BF16)
        for h in range(NP):
            for r in range(0, ROWS, 128):
                block = (lax.broadcasted_iota(jnp.int32, (128, KSEL), 0) + r) * NP + h
                hit = jnp.where(block == names, 1.0, 0.0).astype(BF16)
                mark[h, r : r + 128, :] = jnp.dot(hit, ones, preferred_element_type=F32)

    def store(src, dst):
        c = pltpu.make_async_copy(src, dst, store_sem.at[len(stores)])
        stores.append(c)
        c.start()

    stores = []

    def adam(h, sib_c, c):
        sib_c[3].wait_recv()
        for n in (2, 3, 4, 5):
            c[n].wait_recv()
        cols = slice(h * W, (h + 1) * W)

        for d in range(0, ROWS, 128):
            s = slice(d, d + 128)
            total = (
                part[h, 7, :, s].astype(F32) + sib_in[h, 3, :, s].astype(F32)
                + fin[h, 1, :, s].astype(F32) + fin[h, 2, :, s].astype(F32)
            )
            grad_t[s, :] = jnp.transpose(total, (1, 0))

        def body(n, _):
            s = pl.ds(pl.multiple_of(n * 32, 32), 32)
            g = grad_t[s, :]
            first_new = beta_first * first[s, cols] + (1.0 - beta_first) * g
            second_new = beta_second * second[s, cols] + (1.0 - beta_second) * g * g
            master = wts[7, s, cols].astype(F32)
            stepped = master - inner_rate * (
                first_new / (jnp.sqrt(second_new) + epsilon) + decay_rate * master
            )
            combined = feed[s, cols] + (anchor[s, cols] - stepped)
            marked = mark[h, s, :] > 0.5
            feed_v[h, s, :] = jnp.where(marked, 0.0, combined)
            outg[h, s, :] = jnp.where(marked, combined, 0.0).astype(BF16)
            return 0

        lax.fori_loop(0, ROWS // 32, body, 0)
        store(feed_v.at[h], feed_out.at[0, :, pl.ds(h * W, W)])
        copies = []
        for k in range(1, NY):
            to = lax.rem(y + k, NY)
            c = remote(
                outg.at[h, pl.ds(pl.multiple_of(to * YR, YR), YR)], ybuf.at[h, k - 1],
                y_s.at[h, k - 1], y_r.at[h, k - 1], on_y(k),
            )
            c.start()
            copies.append(c)
        return copies

    def sync_z(h, c):
        for one in c:
            one.wait_recv()
        total = outg[h, pl.ds(pl.multiple_of(y * YR, YR), YR), :].astype(F32)
        for k in range(NY - 1):
            total = total + ybuf[h, k].astype(F32)
        zsrc[h] = total.astype(BF16)
        copies = []
        for k in range(1, NZ):
            to = lax.rem(z + k, NZ)
            c = remote(
                zsrc.at[h, pl.ds(pl.multiple_of(to * ZR, ZR), ZR)], zbuf.at[h, k - 1],
                z_s.at[h, k - 1], z_r.at[h, k - 1], on_z(k),
            )
            c.start()
            copies.append(c)
        return copies

    def gather_z(h, c):
        for one in c:
            one.wait_recv()
        total = zsrc[h, pl.ds(pl.multiple_of(z * ZR, ZR), ZR), :].astype(F32)
        for k in range(NZ - 1):
            total = total + zbuf[h, k].astype(F32)
        mine = pl.ds(pl.multiple_of(y * YR + z * ZR, ZR), ZR)
        avg[h, mine, :] = (total * (1.0 / (NY * NZ))).astype(BF16)
        copies = []
        for k in range(1, NZ):
            c = remote(avg.at[h, mine], avg.at[h, mine], gz_s.at[h, k - 1], gz_r.at[h, k - 1], on_z(k))
            c.start()
            copies.append(c)
        return copies

    def gather_y(h, c):
        for one in c:
            one.wait_recv()
        mine = pl.ds(pl.multiple_of(y * YR, YR), YR)
        copies = []
        for k in range(1, NY):
            c = remote(avg.at[h, mine], avg.at[h, mine], gy_s.at[h, k - 1], gy_r.at[h, k - 1], on_y(k))
            c.start()
            copies.append(c)
        return copies

    def outer(h, c):
        for one in c:
            one.wait_recv()
        cols = slice(h * W, (h + 1) * W)

        def body(n, _):
            s = pl.ds(pl.multiple_of(n * 32, 32), 32)
            average = avg[h, s, :].astype(F32)
            momentum_new = outer_momentum * mom[s, cols] + average
            mom_v[h, s, :] = momentum_new
            anchor_v[h, s, :] = anchor[s, cols] - outer_rate * (average + outer_momentum * momentum_new)
            return 0

        lax.fori_loop(0, ROWS // 32, body, 0)
        store(mom_v.at[h], mom_out.at[:, pl.ds(h * W, W)])
        store(anchor_v.at[h], anchor_out.at[:, pl.ds(h * W, W)])

    def key_block(slot, rows, size, begin=False):
        def body(n, _):
            s = pl.ds(pl.multiple_of(n * 128, 128), 128)
            p = jnp.dot(
                tok[slot, s, rows : rows + size], wts[slot, rows : rows + size, :], preferred_element_type=F32
            )
            acc[s, :] = p if begin else acc[s, :] + p
            return 0

        lax.fori_loop(0, TOK // 128, body, 0)

    def relay(n, slot, rows, size):
        c = remote(
            wts.at[slot, pl.ds(rows, size)], wts.at[slot - 1, pl.ds(rows, size)], rel_s.at[n], rel_r.at[n], sib
        )
        c.start()
        return c

    sib0 = products(0)
    x0 = x_first(0, sib0)
    sib1 = products(1)
    x0 = x_second(0, x0)
    x1 = x_first(1, sib1)
    rel = [relay(0, 7, 0, ROWS)]
    marks()
    for one in l_state:
        one.wait()
    key_block(7, 0, ROWS, begin=True)
    y0 = adam(0, sib0, x0)
    x1 = x_second(1, x1)

    ag_plus_b = ag(2, 7, 256, 5, 1)
    ag_minus_a = ag(3, 7, 0, 3, 3)
    ag_plus_a.wait_recv()
    ag_plus_f = ag(4, 5, 0, 1, 1)
    rel.append(relay(1, 5, 0, 256))
    ag_minus_b.wait_recv()
    ag_minus_f = ag(5, 3, 256, 1, 3)
    rel.append(relay(2, 3, 256, 256))

    z0 = sync_z(0, y0)
    y1 = adam(1, sib1, x1)
    gz0 = gather_z(0, z0)
    rel[0].wait_recv()
    key_block(6, 0, ROWS)
    z1 = sync_z(1, y1)
    gy0 = gather_y(0, gz0)
    gz1 = gather_z(1, z1)
    outer(0, gy0)
    gy1 = gather_y(1, gz1)
    ag_plus_b.wait_recv()
    rel.append(relay(3, 5, 256, 256))
    ag_minus_a.wait_recv()
    rel.append(relay(4, 3, 0, 256))
    key_block(5, 0, ROWS)
    key_block(3, 0, ROWS)
    outer(1, gy1)
    ag_plus_f.wait_recv()
    rel.append(relay(5, 1, 0, 256))
    ag_minus_f.wait_recv()
    rel.append(relay(6, 1, 256, 256))
    key_block(1, 0, ROWS)
    for n in (1, 3):
        rel[n].wait_recv()
    key_block(4, 0, ROWS)
    for n in (2, 4):
        rel[n].wait_recv()
    key_block(2, 0, ROWS)
    for n in (5, 6):
        rel[n].wait_recv()
    key_block(0, 0, ROWS)
    key_v[...] = (acc[...] * (1.0 / math.sqrt(D))).astype(BF16)
    store(key_v, key_hbm)

    ags = [ag_plus_a, ag_minus_b, ag_plus_b, ag_minus_a, ag_plus_f, ag_minus_f]
    for one in sib0 + sib1 + x0 + x1 + y0 + y1 + z0 + z1 + gz0 + gz1 + gy0 + gy1 + ags + rel:
        one.wait_send()
    for one in stores:
        one.wait()


def shards(
    tokens,
    cotangent,
    inner_params,
    first_moment,
    second_moment,
    anchor,
    feedback,
    momentum,
    sel_blocks,
    sel_count,
):
    dma = pltpu.SemaphoreType.DMA
    any_space = pl.BlockSpec(memory_space=pl.ANY)
    return pl.pallas_call(
        kernel,
        out_shape=(
            jax.ShapeDtypeStruct((TOK, COLS), BF16),
            jax.ShapeDtypeStruct((ROWS, COLS), F32),
            jax.ShapeDtypeStruct((1, ROWS, COLS), F32),
            jax.ShapeDtypeStruct((ROWS, COLS), F32),
        ),
        in_specs=[any_space] * 10,
        out_specs=(any_space,) * 4,
        scratch_shapes=[
            pltpu.VMEM((8, TOK, ROWS), BF16),
            pltpu.VMEM((TOK, COLS), BF16),
            pltpu.VMEM((COLS, TOK), BF16),
            pltpu.VMEM((8, ROWS, COLS), BF16),
            pltpu.VMEM((ROWS, COLS), F32),
            pltpu.VMEM((ROWS, COLS), F32),
            pltpu.VMEM((ROWS, COLS), F32),
            pltpu.VMEM((ROWS, COLS), F32),
            pltpu.VMEM((ROWS, COLS), F32),
            pltpu.VMEM((1, KSEL), jnp.int32),
            pltpu.VMEM((1, 1), jnp.int32),
            pltpu.VMEM((NP, 8, W, ROWS), BF16),
            pltpu.VMEM((NP, 4, W, ROWS), BF16),
            pltpu.VMEM((NP, 6, HALF, ROWS), BF16),
            pltpu.VMEM((NP, 3, W, ROWS), BF16),
            pltpu.VMEM((ROWS, W), F32),
            pltpu.VMEM((NP, ROWS, W), F32),
            pltpu.VMEM((NP, ROWS, W), BF16),
            pltpu.VMEM((NP, NY - 1, YR, W), BF16),
            pltpu.VMEM((NP, YR, W), BF16),
            pltpu.VMEM((NP, NZ - 1, ZR, W), BF16),
            pltpu.VMEM((NP, ROWS, W), BF16),
            pltpu.VMEM((TOK, COLS), F32),
            pltpu.VMEM((TOK, COLS), BF16),
            pltpu.VMEM((NP, ROWS, W), F32),
            pltpu.VMEM((NP, ROWS, W), F32),
            pltpu.VMEM((NP, ROWS, W), F32),
            dma((17,)),
            dma((7,)),
            dma((NP, 4)),
            dma((NP, 4)),
            dma((NP, 6)),
            dma((NP, 6)),
            dma((6,)),
            dma((6,)),
            dma((7,)),
            dma((7,)),
            dma((NP, NY - 1)),
            dma((NP, NY - 1)),
            dma((NP, NZ - 1)),
            dma((NP, NZ - 1)),
            dma((NP, NZ - 1)),
            dma((NP, NZ - 1)),
            dma((NP, NY - 1)),
            dma((NP, NY - 1)),
        ],
        compiler_params=pltpu.CompilerParams(
            collective_id=0, has_side_effects=True, vmem_limit_bytes=50 * 1024 * 1024
        ),
        cost_estimate=pl.CostEstimate(flops=4 * TOK * D * COLS, bytes_accessed=14 * 2**20, transcendentals=0),
    )(
        tokens, cotangent, inner_params, first_moment, second_moment, anchor, feedback, momentum,
        sel_blocks.reshape(1, KSEL), sel_count.reshape(1, 1),
    )


def solution(mesh):
    placed = (
        P(("rep", "fsdp"), None),
        P(("rep", "fsdp"), None),
        P("rep", "fsdp", None),
        P("rep", "fsdp", None),
        P("rep", "fsdp", None),
        P("fsdp", None),
        P("rep", "fsdp", None),
        P("fsdp", None),
        P("rep", "fsdp", None),
        P("rep", "fsdp"),
    )
    return jax.shard_map(
        shards,
        mesh=mesh,
        in_specs=placed,
        out_specs=(
            P(("rep", "fsdp"), None),
            P("fsdp", None),
            P("rep", "fsdp", None),
            P("fsdp", None),
        ),
        check_vma=False,
    )
```

```python
import math

import jax
import jax.numpy as jnp
from jax import lax
from jax.experimental import pallas as pl
from jax.experimental.pallas import tpu as pltpu
from jax.sharding import PartitionSpec as P

D = 4096
BLK = 256
COLS = 512
ROWS = 512
TOK = 512
KSEL = 256
NX = 4
NY = 4
NZ = 8
NP = 4
W = COLS // NP
PW = 256
HALF = W // 2
YR = ROWS // NY
ZR = YR // NZ

beta_first = 0.9
beta_second = 0.95
epsilon = 1e-08
decay_rate = 0.1
inner_rate = 1.0
outer_rate = 0.7
outer_momentum = 0.9

MESH = pl.DeviceIdType.MESH
F32 = jnp.float32
BF16 = jnp.bfloat16

ORDER = (2, 1, 3, 0)


def kernel(
    tok_hbm, cot_hbm, par_hbm, first_hbm, second_hbm, anchor_hbm, feed_hbm, mom_hbm, sel_hbm, cnt_hbm,
    key_hbm, anchor_out, feed_out, mom_out,
    tok, cot, cot_t, wts, first, second, anchor, feed, mom, sel, cnt,
    part, sib_in, msg, fin, mark, outg, ybuf, zsrc, zbuf, avg,
    acc, key_v, anchor_v, feed_v, mom_v,
    load_sem, store_sem,
    sib_s, sib_r, x_s, x_r, ag_s, ag_r, rel_s, rel_r,
    y_s, y_r, z_s, z_r, gz_s, gz_r, gy_s, gy_r,
):
    rep = lax.axis_index("rep")
    fs = lax.axis_index("fsdp")
    core = lax.rem(fs, 2)
    x = fs // 2
    y = lax.rem(rep, NY)
    z = rep // NY

    def on_x(k):
        return (rep, lax.rem(x + k, NX) * 2 + core)

    def on_y(k):
        return (z * NY + lax.rem(y + k, NY), fs)

    def on_z(k):
        return (lax.rem(z + k, NZ) * NY + y, fs)

    sib = (rep, x * 2 + 1 - core)

    def remote(src, dst, send, recv, dev):
        return pltpu.make_async_remote_copy(
            src_ref=src, dst_ref=dst, send_sem=send, recv_sem=recv, device_id=dev, device_id_type=MESH
        )

    loads = []

    def load(src, dst):
        c = pltpu.make_async_copy(src, dst, load_sem.at[len(loads)])
        loads.append(c)
        c.start()
        return c

    l_cot = load(cot_hbm, cot)
    l_w = load(par_hbm.at[0], wts.at[7])
    l_tok = []
    for i in range(8):
        chip = lax.rem(x + ORDER[i // 2], NX)
        shard = chip * 2 + (1 - core if i % 2 == 0 else core)
        l_tok.append(load(tok_hbm.at[:, pl.ds(pl.multiple_of(shard * ROWS, ROWS), ROWS)], tok.at[i]))
    l_sel = load(sel_hbm, sel)
    l_cnt = load(cnt_hbm, cnt)
    l_state = [
        load(first_hbm.at[0], first),
        load(second_hbm.at[0], second),
        load(anchor_hbm, anchor),
        load(feed_hbm.at[0], feed),
        load(mom_hbm, mom),
    ]

    barrier = pltpu.get_barrier_semaphore()
    peers = [sib, on_x(1), on_x(3)] + [on_y(k) for k in range(1, NY)] + [on_z(k) for k in range(1, NZ)]
    for dev in peers:
        pl.semaphore_signal(barrier, inc=1, device_id=dev, device_id_type=MESH)

    l_cot.wait()
    cot_t[...] = jnp.transpose(cot[...], (1, 0))
    l_w.wait()
    pl.semaphore_wait(barrier, len(peers))

    ags = []

    def ag(src_slot, dst_slot, rows, size, k):
        n = len(ags)
        c = remote(
            wts.at[src_slot, pl.ds(rows, size)], wts.at[dst_slot, pl.ds(rows, size)], ag_s.at[n], ag_r.at[n], on_x(k)
        )
        c.start()
        ags.append(c)
        return c

    plus = [ag(7, 5, 0, 128, 1)]
    minus = [ag(7, 3, 256, 128, 3)]

    def products(h):
        def body(i, _):
            p = lax.dot_general(
                cot_t[h * PW : (h + 1) * PW, :], tok[i], (((1,), (0,)), ((), ())), preferred_element_type=F32
            )
            part[h, i] = (p * (1.0 / math.sqrt(D))).astype(BF16)
            return 0

        copies = []
        for i in range(8):
            if h == 0:
                l_tok[i].wait()
            body(i, 0)
            if i % 2 == 0:
                c = remote(part.at[h, i], sib_in.at[h, i // 2], sib_s.at[h, i // 2], sib_r.at[h, i // 2], sib)
                c.start()
                copies.append(c)
        return copies

    def x_send(h, n, src, dst, k):
        c = remote(src, dst, x_s.at[h, n], x_r.at[h, n], on_x(k))
        c.start()
        return c

    def pair_sum(h, i, rows):
        s = slice(h % 2 * W + rows, h % 2 * W + rows + HALF)
        return part[h // 2, 2 * i + 1, s, :].astype(F32) + sib_in[h // 2, i, s, :].astype(F32)

    A, B = 0, HALF

    def x_first(h, sib_c):
        if h % 2 == 0:
            sib_c[0].wait_recv()
        msg[h, 0] = pair_sum(h, 0, A).astype(BF16)
        c0 = x_send(h, 0, msg.at[h, 0], fin.at[h, 0, pl.ds(A, HALF)], 1)
        msg[h, 1] = pair_sum(h, 0, B).astype(BF16)
        c1 = x_send(h, 1, msg.at[h, 1], fin.at[h, 0, pl.ds(B, HALF)], 3)
        if h % 2 == 0:
            sib_c[1].wait_recv()
        msg[h, 2] = pair_sum(h, 1, B).astype(BF16)
        c2 = x_send(h, 2, msg.at[h, 2], fin.at[h, 1, pl.ds(B, HALF)], 1)
        if h % 2 == 0:
            sib_c[2].wait_recv()
        msg[h, 3] = pair_sum(h, 2, A).astype(BF16)
        c3 = x_send(h, 3, msg.at[h, 3], fin.at[h, 2, pl.ds(A, HALF)], 3)
        return [c0, c1, c2, c3]

    def x_second(h, c):
        c[0].wait_recv()
        msg[h, 4] = (pair_sum(h, 1, A) + fin[h, 0, A : A + HALF, :].astype(F32)).astype(BF16)
        c4 = x_send(h, 4, msg.at[h, 4], fin.at[h, 1, pl.ds(A, HALF)], 1)
        c[1].wait_recv()
        msg[h, 5] = (pair_sum(h, 2, B) + fin[h, 0, B : B + HALF, :].astype(F32)).astype(BF16)
        c5 = x_send(h, 5, msg.at[h, 5], fin.at[h, 2, pl.ds(B, HALF)], 3)
        return c + [c4, c5]

    def marks():
        l_sel.wait()
        l_cnt.wait()
        place = lax.broadcasted_iota(jnp.int32, (1, KSEL), 1)
        names = jnp.where(place < cnt[...], sel[...], -1)
        ones = jnp.ones((KSEL, W), BF16)
        for b in range(COLS // BLK):
            for r in range(0, ROWS, 128):
                block = (lax.broadcasted_iota(jnp.int32, (128, KSEL), 0) + r) * (COLS // BLK) + b
                hit = jnp.where(block == names, 1.0, 0.0).astype(BF16)
                mark[b, r : r + 128, :] = jnp.dot(hit, ones, preferred_element_type=F32)

    def store(src, dst):
        c = pltpu.make_async_copy(src, dst, store_sem.at[len(stores)])
        stores.append(c)
        c.start()

    stores = []

    def adam(h, sib_c, c):
        if h % 2 == 0:
            sib_c[3].wait_recv()
        for n in (2, 3, 4, 5):
            c[n].wait_recv()
        cols = slice(h * W, (h + 1) * W)
        half = slice(h % 2 * W, h % 2 * W + W)

        def body(n, _):
            s = pl.ds(pl.multiple_of(n * 128, 128), 128)
            total = (
                part[h // 2, 7, half, s].astype(F32) + sib_in[h // 2, 3, half, s].astype(F32)
                + fin[h, 1, :, s].astype(F32) + fin[h, 2, :, s].astype(F32)
            )
            gradient = jnp.transpose(total, (1, 0))
            for r in range(0, 128, 32):
                s = pl.ds(pl.multiple_of(n * 128 + r, 32), 32)
                g = gradient[r : r + 32, :]
                first_new = beta_first * first[s, cols] + (1.0 - beta_first) * g
                second_new = beta_second * second[s, cols] + (1.0 - beta_second) * g * g
                master = wts[7, s, cols].astype(F32)
                stepped = master - inner_rate * (
                    first_new / (jnp.sqrt(second_new) + epsilon) + decay_rate * master
                )
                combined = feed[s, cols] + (anchor[s, cols] - stepped)
                marked = mark[h * W // BLK, s, :] > 0.5
                feed_v[h, s, :] = jnp.where(marked, 0.0, combined)
                outg[h, s, :] = jnp.where(marked, combined, 0.0).astype(BF16)
            return 0

        lax.fori_loop(0, ROWS // 128, body, 0)
        store(feed_v.at[h], feed_out.at[0, :, pl.ds(h * W, W)])
        copies = []
        for k in range(1, NY):
            to = lax.rem(y + k, NY)
            c = remote(
                outg.at[h, pl.ds(pl.multiple_of(to * YR, YR), YR)], ybuf.at[h, k - 1],
                y_s.at[h, k - 1], y_r.at[h, k - 1], on_y(k),
            )
            c.start()
            copies.append(c)
        return copies

    def sync_z(h, c):
        for one in c:
            one.wait_recv()
        total = outg[h, pl.ds(pl.multiple_of(y * YR, YR), YR), :].astype(F32)
        for k in range(NY - 1):
            total = total + ybuf[h, k].astype(F32)
        zsrc[h] = total.astype(BF16)
        copies = []
        for k in range(1, NZ):
            to = lax.rem(z + k, NZ)
            c = remote(
                zsrc.at[h, pl.ds(pl.multiple_of(to * ZR, ZR), ZR)], zbuf.at[h, k - 1],
                z_s.at[h, k - 1], z_r.at[h, k - 1], on_z(k),
            )
            c.start()
            copies.append(c)
        return copies

    def gather_z(h, c):
        for one in c:
            one.wait_recv()
        total = zsrc[h, pl.ds(pl.multiple_of(z * ZR, ZR), ZR), :].astype(F32)
        for k in range(NZ - 1):
            total = total + zbuf[h, k].astype(F32)
        mine = pl.ds(pl.multiple_of(y * YR + z * ZR, ZR), ZR)
        avg[h, mine, :] = (total * (1.0 / (NY * NZ))).astype(BF16)
        copies = []
        for k in range(1, NZ):
            c = remote(avg.at[h, mine], avg.at[h, mine], gz_s.at[h, k - 1], gz_r.at[h, k - 1], on_z(k))
            c.start()
            copies.append(c)
        return copies

    def gather_y(h, c):
        for one in c:
            one.wait_recv()
        mine = pl.ds(pl.multiple_of(y * YR, YR), YR)
        copies = []
        for k in range(1, NY):
            c = remote(avg.at[h, mine], avg.at[h, mine], gy_s.at[h, k - 1], gy_r.at[h, k - 1], on_y(k))
            c.start()
            copies.append(c)
        return copies

    def outer(h, c):
        for one in c:
            one.wait_recv()
        cols = slice(h * W, (h + 1) * W)

        def body(n, _):
            s = pl.ds(pl.multiple_of(n * 32, 32), 32)
            average = avg[h, s, :].astype(F32)
            momentum_new = outer_momentum * mom[s, cols] + average
            mom_v[h, s, :] = momentum_new
            anchor_v[h, s, :] = anchor[s, cols] - outer_rate * (average + outer_momentum * momentum_new)
            return 0

        lax.fori_loop(0, ROWS // 32, body, 0)
        store(mom_v.at[h], mom_out.at[:, pl.ds(h * W, W)])
        store(anchor_v.at[h], anchor_out.at[:, pl.ds(h * W, W)])

    def key_block(slots, begin=False):
        p = None if begin else acc[...]
        for slot in slots:
            q = jnp.dot(tok[slot], wts[slot], preferred_element_type=F32)
            p = q if p is None else p + q
        acc[...] = p

    rel = []

    def relay(slot, rows, size):
        n = len(rel)
        c = remote(
            wts.at[slot, pl.ds(rows, size)], wts.at[slot - 1, pl.ds(rows, size)], rel_s.at[n], rel_r.at[n], sib
        )
        c.start()
        rel.append(c)

    xs, ys, zs, gzs, gys = [None] * NP, [None] * NP, [None] * NP, [None] * NP, [None] * NP
    sibs = [products(0)]
    xs[0] = x_first(0, sibs[0])
    xs[1] = x_first(1, sibs[0])
    sibs.append(products(1))
    xs[0] = x_second(0, xs[0])
    xs[2] = x_first(2, sibs[1])
    relay(7, 0, ROWS)
    marks()
    for one in l_state:
        one.wait()
    xs[1] = x_second(1, xs[1])
    xs[3] = x_first(3, sibs[1])
    ys[0] = adam(0, sibs[0], xs[0])
    xs[2] = x_second(2, xs[2])
    rel[0].wait_recv()
    key_block((7, 6), begin=True)
    ys[1] = adam(1, sibs[0], xs[1])
    zs[0] = sync_z(0, ys[0])
    xs[3] = x_second(3, xs[3])
    ys[2] = adam(2, sibs[1], xs[2])
    zs[1] = sync_z(1, ys[1])
    gzs[0] = gather_z(0, zs[0])
    ys[3] = adam(3, sibs[1], xs[3])

    plus[0].wait_recv()
    minus[0].wait_recv()
    plus += [ag(7, 5, 128, 128, 1), ag(5, 1, 0, 128, 1), ag(7, 5, 256, 256, 1)]
    minus += [ag(7, 3, 384, 128, 3), ag(3, 1, 256, 128, 3), ag(7, 3, 0, 256, 3)]
    relay(5, 0, 128)
    relay(3, 256, 128)

    zs[2] = sync_z(2, ys[2])
    gzs[1] = gather_z(1, zs[1])
    gys[0] = gather_y(0, gzs[0])
    zs[3] = sync_z(3, ys[3])
    plus[1].wait_recv()
    minus[1].wait_recv()
    plus += [ag(5, 1, 128, 128, 1)]
    minus += [ag(3, 1, 384, 128, 3)]
    relay(5, 128, 128)
    relay(3, 384, 128)
    gzs[2] = gather_z(2, zs[2])
    gys[1] = gather_y(1, gzs[1])
    outer(0, gys[0])
    gzs[3] = gather_z(3, zs[3])
    gys[2] = gather_y(2, gzs[2])
    outer(1, gys[1])
    gys[3] = gather_y(3, gzs[3])
    plus[3].wait_recv()
    relay(5, 256, 256)
    minus[3].wait_recv()
    relay(3, 0, 256)
    key_block((5, 3))
    outer(2, gys[2])
    for n in (2, 4):
        plus[n].wait_recv()
        minus[n].wait_recv()
    relay(1, 0, 256)
    relay(1, 256, 256)
    outer(3, gys[3])
    for one in rel[1:7]:
        one.wait_recv()
    key_block((1, 4, 2))
    for one in rel[7:]:
        one.wait_recv()
    key_block((0,))
    key_v[...] = (acc[...] * (1.0 / math.sqrt(D))).astype(BF16)
    store(key_v, key_hbm)

    for group in sibs + xs + ys + zs + gzs + gys + [ags, rel]:
        for one in group:
            one.wait_send()
    for one in stores:
        one.wait()


def flush(*refs):
    sem = refs[-1]
    copies = [pltpu.make_async_copy(refs[n], refs[4 + n], sem.at[n]) for n in range(4)]
    for one in copies:
        one.start()
    for one in copies:
        one.wait()


def shards(
    tokens,
    cotangent,
    inner_params,
    first_moment,
    second_moment,
    anchor,
    feedback,
    momentum,
    sel_blocks,
    sel_count,
):
    dma = pltpu.SemaphoreType.DMA
    any_space = pl.BlockSpec(memory_space=pl.ANY)
    hbm = pl.BlockSpec(memory_space=pltpu.HBM)
    outs = (
            jax.ShapeDtypeStruct((TOK, COLS), BF16),
            jax.ShapeDtypeStruct((ROWS, COLS), F32),
            jax.ShapeDtypeStruct((1, ROWS, COLS), F32),
            jax.ShapeDtypeStruct((ROWS, COLS), F32),
        )
    done = pl.pallas_call(
        kernel,
        out_shape=outs,
        in_specs=[hbm] * 10,
        out_specs=(any_space,) * 4,
        scratch_shapes=[
            pltpu.VMEM((8, TOK, ROWS), BF16),
            pltpu.VMEM((TOK, COLS), BF16),
            pltpu.VMEM((COLS, TOK), BF16),
            pltpu.VMEM((8, ROWS, COLS), BF16),
            pltpu.VMEM((ROWS, COLS), F32),
            pltpu.VMEM((ROWS, COLS), F32),
            pltpu.VMEM((ROWS, COLS), F32),
            pltpu.VMEM((ROWS, COLS), F32),
            pltpu.VMEM((ROWS, COLS), F32),
            pltpu.VMEM((1, KSEL), jnp.int32),
            pltpu.VMEM((1, 1), jnp.int32),
            pltpu.VMEM((COLS // PW, 8, PW, ROWS), BF16),
            pltpu.VMEM((COLS // PW, 4, PW, ROWS), BF16),
            pltpu.VMEM((NP, 6, HALF, ROWS), BF16),
            pltpu.VMEM((NP, 3, W, ROWS), BF16),
            pltpu.VMEM((COLS // BLK, ROWS, W), F32),
            pltpu.VMEM((NP, ROWS, W), BF16),
            pltpu.VMEM((NP, NY - 1, YR, W), BF16),
            pltpu.VMEM((NP, YR, W), BF16),
            pltpu.VMEM((NP, NZ - 1, ZR, W), BF16),
            pltpu.VMEM((NP, ROWS, W), BF16),
            pltpu.VMEM((TOK, COLS), F32),
            pltpu.VMEM((TOK, COLS), BF16),
            pltpu.VMEM((NP, ROWS, W), F32),
            pltpu.VMEM((NP, ROWS, W), F32),
            pltpu.VMEM((NP, ROWS, W), F32),
            dma((17,)),
            dma((3 * NP + 1,)),
            dma((COLS // PW, 4)),
            dma((COLS // PW, 4)),
            dma((NP, 6)),
            dma((NP, 6)),
            dma((10,)),
            dma((10,)),
            dma((11,)),
            dma((11,)),
            dma((NP, NY - 1)),
            dma((NP, NY - 1)),
            dma((NP, NZ - 1)),
            dma((NP, NZ - 1)),
            dma((NP, NZ - 1)),
            dma((NP, NZ - 1)),
            dma((NP, NY - 1)),
            dma((NP, NY - 1)),
        ],
        compiler_params=pltpu.CompilerParams(
            collective_id=0, has_side_effects=True, vmem_limit_bytes=40 * 1024 * 1024
        ),
        cost_estimate=pl.CostEstimate(flops=4 * TOK * D * COLS, bytes_accessed=14 * 2**20, transcendentals=0),
    )(
        *(
            pltpu.with_memory_space_constraint(a, pltpu.HBM)
            for a in (
                tokens, cotangent, inner_params, first_moment, second_moment, anchor, feedback, momentum,
                sel_blocks.reshape(1, KSEL),
            )
        ),
        sel_count.reshape(1, 1),
    )
    return pl.pallas_call(
        flush,
        out_shape=outs,
        in_specs=[any_space] * 4,
        out_specs=(any_space,) * 4,
        scratch_shapes=[dma((4,))],
        compiler_params=pltpu.CompilerParams(has_side_effects=True, vmem_limit_bytes=4 * 1024 * 1024),
    )(*done)


def solution(mesh):
    placed = (
        P(("rep", "fsdp"), None),
        P(("rep", "fsdp"), None),
        P("rep", "fsdp", None),
        P("rep", "fsdp", None),
        P("rep", "fsdp", None),
        P("fsdp", None),
        P("rep", "fsdp", None),
        P("fsdp", None),
        P("rep", "fsdp", None),
        P("rep", "fsdp"),
    )
    return jax.shard_map(
        shards,
        mesh=mesh,
        in_specs=placed,
        out_specs=(
            P(("rep", "fsdp"), None),
            P("fsdp", None),
            P("rep", "fsdp", None),
            P("fsdp", None),
        ),
        check_vma=False,
    )
```

```python
import math

import jax
import jax.numpy as jnp
from jax import lax
from jax.experimental import pallas as pl
from jax.experimental.pallas import tpu as pltpu
from jax.sharding import PartitionSpec as P

D = 4096
BLK = 256
COLS = 512
ROWS = 512
TOK = 512
KSEL = 256
NX = 4
NY = 4
NZ = 8
NP = 4
W = COLS // NP
PW = 256
HALF = W // 2
YR = ROWS // NY
ZR = YR // NZ

beta_first = 0.9
beta_second = 0.95
epsilon = 1e-08
decay_rate = 0.1
inner_rate = 1.0
outer_rate = 0.7
outer_momentum = 0.9

MESH = pl.DeviceIdType.MESH
F32 = jnp.float32
BF16 = jnp.bfloat16

ORDER = (2, 1, 3, 0)
FAR_FIRST = (4, 3, 5, 2, 6, 1, 7)


def kernel(
    tok_hbm, cot_hbm, par_hbm, first_hbm, second_hbm, anchor_hbm, feed_hbm, mom_hbm, sel_hbm, cnt_hbm,
    key_hbm, anchor_out, feed_out, mom_out,
    tok, cot, cot_t, wts, first, second, anchor, feed, mom, sel, cnt,
    part, sib_in, msg, fin, mark, outg, ybuf, zsrc, zbuf, avg,
    acc, key_v, anchor_v, feed_v, mom_v,
    load_sem, store_sem,
    sib_s, sib_r, x_s, x_r, ag_s, ag_r, rel_s, rel_r,
    y_s, y_r, z_s, z_r, gz_s, gz_r, gy_s, gy_r,
):
    rep = lax.axis_index("rep")
    fs = lax.axis_index("fsdp")
    core = lax.rem(fs, 2)
    x = fs // 2
    y = lax.rem(rep, NY)
    z = rep // NY

    def on_x(k):
        return (rep, lax.rem(x + k, NX) * 2 + core)

    def on_y(k):
        return (z * NY + lax.rem(y + k, NY), fs)

    def on_z(k):
        return (lax.rem(z + k, NZ) * NY + y, fs)

    sib = (rep, x * 2 + 1 - core)

    def remote(src, dst, send, recv, dev):
        return pltpu.make_async_remote_copy(
            src_ref=src, dst_ref=dst, send_sem=send, recv_sem=recv, device_id=dev, device_id_type=MESH
        )

    loads = []

    def load(src, dst):
        c = pltpu.make_async_copy(src, dst, load_sem.at[len(loads)])
        loads.append(c)
        c.start()
        return c

    def load_tok(i):
        chip = lax.rem(x + ORDER[i // 2], NX)
        shard = chip * 2 + (1 - core if i % 2 == 0 else core)
        return load(tok_hbm.at[:, pl.ds(pl.multiple_of(shard * ROWS, ROWS), ROWS)], tok.at[i])

    l_cot = load(cot_hbm, cot)
    l_tok = [load_tok(0), load_tok(1)]

    barrier = pltpu.get_barrier_semaphore()
    peers = [sib, on_x(1), on_x(3)] + [on_y(k) for k in range(1, NY)] + [on_z(k) for k in range(1, NZ)]
    for dev in peers:
        pl.semaphore_signal(barrier, inc=1, device_id=dev, device_id_type=MESH)

    l_w = load(par_hbm.at[0], wts.at[7])
    l_tok += [load_tok(i) for i in range(2, 8)]
    l_sel = load(sel_hbm, sel)
    l_cnt = load(cnt_hbm, cnt)
    l_state = [
        load(first_hbm.at[0], first),
        load(second_hbm.at[0], second),
        load(anchor_hbm, anchor),
        load(feed_hbm.at[0], feed),
        load(mom_hbm, mom),
    ]
    l_cot.wait()
    cot_t[...] = jnp.transpose(cot[...], (1, 0))

    ags = []

    def ag(src_slot, dst_slot, rows, size, k):
        n = len(ags)
        c = remote(
            wts.at[src_slot, pl.ds(rows, size)], wts.at[dst_slot, pl.ds(rows, size)], ag_s.at[n], ag_r.at[n], on_x(k)
        )
        c.start()
        ags.append(c)
        return c

    def product(i):
        l_tok[i].wait()
        p = jnp.dot(cot_t[...], tok[i], preferred_element_type=F32)
        p = (p * (1.0 / math.sqrt(D))).astype(BF16)
        for h in range(COLS // PW):
            part[h, i] = p[h * PW : (h + 1) * PW, :]

    sibs = [[], []]

    def exchange(h, i):
        c = remote(part.at[h, 2 * i], sib_in.at[h, i], sib_s.at[h, i], sib_r.at[h, i], sib)
        c.start()
        sibs[h].append(c)

    def x_send(h, n, src, dst, k):
        c = remote(src, dst, x_s.at[h, n], x_r.at[h, n], on_x(k))
        c.start()
        return c

    def pair_sum(h, i, rows):
        s = slice(h % 2 * W + rows, h % 2 * W + rows + HALF)
        return part[h // 2, 2 * i + 1, s, :].astype(F32) + sib_in[h // 2, i, s, :].astype(F32)

    A, B = 0, HALF

    xs = [[] for _ in range(NP)]

    def x_first(h):
        msg[h, 0] = pair_sum(h, 0, A).astype(BF16)
        xs[h].append(x_send(h, 0, msg.at[h, 0], fin.at[h, 0, pl.ds(A, HALF)], 1))
        msg[h, 1] = pair_sum(h, 0, B).astype(BF16)
        xs[h].append(x_send(h, 1, msg.at[h, 1], fin.at[h, 0, pl.ds(B, HALF)], 3))

    def x_plus(h):
        msg[h, 2] = pair_sum(h, 1, B).astype(BF16)
        xs[h].append(x_send(h, 2, msg.at[h, 2], fin.at[h, 1, pl.ds(B, HALF)], 1))

    def x_minus(h):
        msg[h, 3] = pair_sum(h, 2, A).astype(BF16)
        xs[h].append(x_send(h, 3, msg.at[h, 3], fin.at[h, 2, pl.ds(A, HALF)], 3))

    def x_second(h):
        xs[h][0].wait_recv()
        msg[h, 4] = (pair_sum(h, 1, A) + fin[h, 0, A : A + HALF, :].astype(F32)).astype(BF16)
        xs[h].append(x_send(h, 4, msg.at[h, 4], fin.at[h, 1, pl.ds(A, HALF)], 1))
        xs[h][1].wait_recv()
        msg[h, 5] = (pair_sum(h, 2, B) + fin[h, 0, B : B + HALF, :].astype(F32)).astype(BF16)
        xs[h].append(x_send(h, 5, msg.at[h, 5], fin.at[h, 2, pl.ds(B, HALF)], 3))

    def marks():
        l_sel.wait()
        l_cnt.wait()
        place = lax.broadcasted_iota(jnp.int32, (1, KSEL), 1)
        names = jnp.where(place < cnt[...], sel[...], -1)
        ones = jnp.ones((KSEL, W), BF16)
        for b in range(COLS // BLK):
            for r in range(0, ROWS, 128):
                block = (lax.broadcasted_iota(jnp.int32, (128, KSEL), 0) + r) * (COLS // BLK) + b
                hit = jnp.where(block == names, 1.0, 0.0).astype(BF16)
                mark[b, r : r + 128, :] = jnp.dot(hit, ones, preferred_element_type=F32)

    def store(src, dst):
        c = pltpu.make_async_copy(src, dst, store_sem.at[len(stores)])
        stores.append(c)
        c.start()

    stores = []

    def adam(h):
        for n in (2, 3, 4, 5):
            xs[h][n].wait_recv()
        cols = slice(h * W, (h + 1) * W)
        half = slice(h % 2 * W, h % 2 * W + W)
        copies = []
        for k in (2, 1, 3, 0):
            first_row = pl.multiple_of(lax.rem(y + k, NY) * YR, YR)
            block = pl.ds(first_row, YR)
            total = (
                part[h // 2, 7, half, block].astype(F32) + sib_in[h // 2, 3, half, block].astype(F32)
                + fin[h, 1, :, block].astype(F32) + fin[h, 2, :, block].astype(F32)
            )
            gradient = jnp.transpose(total, (1, 0))
            for r in range(0, YR, 32):
                s = pl.ds(pl.multiple_of(first_row + r, 32), 32)
                g = gradient[r : r + 32, :]
                first_new = beta_first * first[s, cols] + (1.0 - beta_first) * g
                second_new = beta_second * second[s, cols] + (1.0 - beta_second) * g * g
                master = wts[7, s, cols].astype(F32)
                stepped = master - inner_rate * (
                    first_new / (jnp.sqrt(second_new) + epsilon) + decay_rate * master
                )
                combined = feed[s, cols] + (anchor[s, cols] - stepped)
                marked = mark[h * W // BLK, s, :] > 0.5
                feed_v[h, s, :] = jnp.where(marked, 0.0, combined)
                outg[h, s, :] = jnp.where(marked, combined, 0.0).astype(BF16)
            if k > 0:
                c = remote(outg.at[h, block], ybuf.at[h, k - 1], y_s.at[h, k - 1], y_r.at[h, k - 1], on_y(k))
                c.start()
                copies.append(c)
        store(feed_v.at[h], feed_out.at[0, :, pl.ds(h * W, W)])
        return copies

    def sync_z(h, c):
        for one in c:
            one.wait_recv()
        total = outg[h, pl.ds(pl.multiple_of(y * YR, YR), YR), :].astype(F32)
        for k in range(NY - 1):
            total = total + ybuf[h, k].astype(F32)
        zsrc[h] = total.astype(BF16)
        copies = []
        for k in FAR_FIRST:
            to = lax.rem(z + k, NZ)
            c = remote(
                zsrc.at[h, pl.ds(pl.multiple_of(to * ZR, ZR), ZR)], zbuf.at[h, k - 1],
                z_s.at[h, k - 1], z_r.at[h, k - 1], on_z(k),
            )
            c.start()
            copies.append(c)
        return copies

    def gather_z(h, c):
        for one in c:
            one.wait_recv()
        total = zsrc[h, pl.ds(pl.multiple_of(z * ZR, ZR), ZR), :].astype(F32)
        for k in range(NZ - 1):
            total = total + zbuf[h, k].astype(F32)
        mine = pl.ds(pl.multiple_of(y * YR + z * ZR, ZR), ZR)
        avg[h, mine, :] = (total * (1.0 / (NY * NZ))).astype(BF16)
        copies = []
        for k in FAR_FIRST:
            c = remote(avg.at[h, mine], avg.at[h, mine], gz_s.at[h, k - 1], gz_r.at[h, k - 1], on_z(k))
            c.start()
            copies.append(c)
        return copies

    def gather_y(h, c):
        for one in c:
            one.wait_recv()
        mine = pl.ds(pl.multiple_of(y * YR, YR), YR)
        copies = []
        for k in range(1, NY):
            c = remote(avg.at[h, mine], avg.at[h, mine], gy_s.at[h, k - 1], gy_r.at[h, k - 1], on_y(k))
            c.start()
            copies.append(c)
        return copies

    def outer(h, c):
        for one in c:
            one.wait_recv()
        cols = slice(h * W, (h + 1) * W)

        def body(n, _):
            s = pl.ds(pl.multiple_of(n * 32, 32), 32)
            average = avg[h, s, :].astype(F32)
            momentum_new = outer_momentum * mom[s, cols] + average
            mom_v[h, s, :] = momentum_new
            anchor_v[h, s, :] = anchor[s, cols] - outer_rate * (average + outer_momentum * momentum_new)
            return 0

        lax.fori_loop(0, ROWS // 32, body, 0)
        store(mom_v.at[h], mom_out.at[:, pl.ds(h * W, W)])
        store(anchor_v.at[h], anchor_out.at[:, pl.ds(h * W, W)])

    def key_block(slots, begin=False):
        p = None if begin else acc[...]
        for slot in slots:
            q = jnp.dot(tok[slot], wts[slot], preferred_element_type=F32)
            p = q if p is None else p + q
        acc[...] = p

    rel = []

    def relay(slot, rows, size):
        n = len(rel)
        c = remote(
            wts.at[slot, pl.ds(rows, size)], wts.at[slot - 1, pl.ds(rows, size)], rel_s.at[n], rel_r.at[n], sib
        )
        c.start()
        rel.append(c)

    ys, zs, gzs, gys = [None] * NP, [None] * NP, [None] * NP, [None] * NP
    product(0)
    pl.semaphore_wait(barrier, len(peers))
    exchange(0, 0)
    exchange(1, 0)
    l_w.wait()
    plus = [ag(7, 5, 0, 64, 1)]
    minus = [ag(7, 3, 256, 64, 3)]
    product(1)
    product(2)
    exchange(0, 1)
    product(3)
    sibs[0][0].wait_recv()
    x_first(0)
    x_first(1)
    product(4)
    exchange(0, 2)
    exchange(1, 1)
    exchange(1, 2)
    sibs[1][0].wait_recv()
    x_first(2)
    x_first(3)
    sibs[0][1].wait_recv()
    x_plus(0)
    product(5)
    sibs[0][2].wait_recv()
    x_minus(0)
    x_second(0)
    x_plus(1)
    x_minus(1)
    product(6)
    exchange(0, 3)
    exchange(1, 3)
    x_second(1)
    sibs[1][1].wait_recv()
    x_plus(2)
    sibs[1][2].wait_recv()
    x_minus(2)
    product(7)
    x_second(2)
    x_plus(3)
    x_minus(3)
    marks()
    x_second(3)
    relay(7, 0, ROWS)
    plus += [ag(7, 5, 64, 192, 1)]
    minus += [ag(7, 3, 320, 192, 3)]
    plus[0].wait_recv()
    minus[0].wait_recv()
    plus += [ag(5, 1, 0, 64, 1), ag(7, 5, 256, 256, 1)]
    minus += [ag(3, 1, 256, 64, 3), ag(7, 3, 0, 256, 3)]
    relay(5, 0, 64)
    relay(3, 256, 64)
    for one in l_state:
        one.wait()
    sibs[0][3].wait_recv()
    ys[0] = adam(0)
    rel[0].wait_recv()
    key_block((7, 6), begin=True)
    ys[1] = adam(1)
    zs[0] = sync_z(0, ys[0])
    sibs[1][3].wait_recv()
    ys[2] = adam(2)
    zs[1] = sync_z(1, ys[1])
    ys[3] = adam(3)

    zs[2] = sync_z(2, ys[2])
    zs[3] = sync_z(3, ys[3])
    plus[1].wait_recv()
    plus.append(ag(5, 1, 64, 192, 1))
    minus[1].wait_recv()
    minus.append(ag(3, 1, 320, 192, 3))
    relay(5, 64, 192)
    relay(3, 320, 192)
    gzs[0] = gather_z(0, zs[0])
    gzs[1] = gather_z(1, zs[1])
    plus[2].wait_recv()
    relay(1, 0, 64)
    minus[2].wait_recv()
    relay(1, 256, 64)
    gzs[2] = gather_z(2, zs[2])
    gzs[3] = gather_z(3, zs[3])
    for h in range(NP - 1):
        gys[h] = gather_y(h, gzs[h])
    plus[3].wait_recv()
    relay(5, 256, 256)
    minus[3].wait_recv()
    relay(3, 0, 256)
    key_block((5, 3))
    gys[3] = gather_y(3, gzs[3])
    outer(0, gys[0])
    plus[4].wait_recv()
    relay(1, 64, 192)
    minus[4].wait_recv()
    relay(1, 320, 192)
    key_block((1,))
    outer(1, gys[1])
    outer(2, gys[2])
    for one in rel[1:]:
        one.wait_recv()
    key_block((4, 2, 0))
    key_v[...] = (acc[...] * (1.0 / math.sqrt(D))).astype(BF16)
    store(key_v, key_hbm)
    outer(3, gys[3])

    for group in sibs + xs + ys + zs + gzs + gys + [ags, rel]:
        for one in group:
            one.wait_send()
    for one in stores:
        one.wait()


def flush(*refs):
    sem = refs[-1]
    copies = [pltpu.make_async_copy(refs[n], refs[4 + n], sem.at[n]) for n in range(4)]
    for one in copies:
        one.start()
    for one in copies:
        one.wait()


def shards(
    tokens,
    cotangent,
    inner_params,
    first_moment,
    second_moment,
    anchor,
    feedback,
    momentum,
    sel_blocks,
    sel_count,
):
    dma = pltpu.SemaphoreType.DMA
    any_space = pl.BlockSpec(memory_space=pl.ANY)
    hbm = pl.BlockSpec(memory_space=pltpu.HBM)
    outs = (
            jax.ShapeDtypeStruct((TOK, COLS), BF16),
            jax.ShapeDtypeStruct((ROWS, COLS), F32),
            jax.ShapeDtypeStruct((1, ROWS, COLS), F32),
            jax.ShapeDtypeStruct((ROWS, COLS), F32),
        )
    done = pl.pallas_call(
        kernel,
        out_shape=outs,
        in_specs=[hbm] * 10,
        out_specs=(any_space,) * 4,
        scratch_shapes=[
            pltpu.VMEM((8, TOK, ROWS), BF16),
            pltpu.VMEM((TOK, COLS), BF16),
            pltpu.VMEM((COLS, TOK), BF16),
            pltpu.VMEM((8, ROWS, COLS), BF16),
            pltpu.VMEM((ROWS, COLS), F32),
            pltpu.VMEM((ROWS, COLS), F32),
            pltpu.VMEM((ROWS, COLS), F32),
            pltpu.VMEM((ROWS, COLS), F32),
            pltpu.VMEM((ROWS, COLS), F32),
            pltpu.VMEM((1, KSEL), jnp.int32),
            pltpu.VMEM((1, 1), jnp.int32),
            pltpu.VMEM((COLS // PW, 8, PW, ROWS), BF16),
            pltpu.VMEM((COLS // PW, 4, PW, ROWS), BF16),
            pltpu.VMEM((NP, 6, HALF, ROWS), BF16),
            pltpu.VMEM((NP, 3, W, ROWS), BF16),
            pltpu.VMEM((COLS // BLK, ROWS, W), F32),
            pltpu.VMEM((NP, ROWS, W), BF16),
            pltpu.VMEM((NP, NY - 1, YR, W), BF16),
            pltpu.VMEM((NP, YR, W), BF16),
            pltpu.VMEM((NP, NZ - 1, ZR, W), BF16),
            pltpu.VMEM((NP, ROWS, W), BF16),
            pltpu.VMEM((TOK, COLS), F32),
            pltpu.VMEM((TOK, COLS), BF16),
            pltpu.VMEM((NP, ROWS, W), F32),
            pltpu.VMEM((NP, ROWS, W), F32),
            pltpu.VMEM((NP, ROWS, W), F32),
            dma((17,)),
            dma((3 * NP + 1,)),
            dma((COLS // PW, 4)),
            dma((COLS // PW, 4)),
            dma((NP, 6)),
            dma((NP, 6)),
            dma((10,)),
            dma((10,)),
            dma((11,)),
            dma((11,)),
            dma((NP, NY - 1)),
            dma((NP, NY - 1)),
            dma((NP, NZ - 1)),
            dma((NP, NZ - 1)),
            dma((NP, NZ - 1)),
            dma((NP, NZ - 1)),
            dma((NP, NY - 1)),
            dma((NP, NY - 1)),
        ],
        compiler_params=pltpu.CompilerParams(
            collective_id=0, has_side_effects=True, vmem_limit_bytes=40 * 1024 * 1024
        ),
        cost_estimate=pl.CostEstimate(flops=4 * TOK * D * COLS, bytes_accessed=14 * 2**20, transcendentals=0),
    )(
        *(
            pltpu.with_memory_space_constraint(a, pltpu.HBM)
            for a in (
                tokens, cotangent, inner_params, first_moment, second_moment, anchor, feedback, momentum,
                sel_blocks.reshape(1, KSEL),
            )
        ),
        sel_count.reshape(1, 1),
    )
    return pl.pallas_call(
        flush,
        out_shape=outs,
        in_specs=[any_space] * 4,
        out_specs=(any_space,) * 4,
        scratch_shapes=[dma((4,))],
        compiler_params=pltpu.CompilerParams(has_side_effects=True, vmem_limit_bytes=4 * 1024 * 1024),
    )(*done)


def solution(mesh):
    placed = (
        P(("rep", "fsdp"), None),
        P(("rep", "fsdp"), None),
        P("rep", "fsdp", None),
        P("rep", "fsdp", None),
        P("rep", "fsdp", None),
        P("fsdp", None),
        P("rep", "fsdp", None),
        P("fsdp", None),
        P("rep", "fsdp", None),
        P("rep", "fsdp"),
    )
    return jax.shard_map(
        shards,
        mesh=mesh,
        in_specs=placed,
        out_specs=(
            P(("rep", "fsdp"), None),
            P("fsdp", None),
            P("rep", "fsdp", None),
            P("fsdp", None),
        ),
        check_vma=False,
    )
```

```python
import math

import jax
import jax.numpy as jnp
from jax import lax
from jax.experimental import pallas as pl
from jax.experimental.pallas import tpu as pltpu
from jax.sharding import PartitionSpec as P

D = 4096
BLK = 256
COLS = 512
ROWS = 512
TOK = 512
KSEL = 256
NX = 4
NY = 4
NZ = 8
NP = 4
W = COLS // NP
PW = 256
HALF = W // 2
YR = ROWS // NY
ZR = YR // NZ

beta_first = 0.9
beta_second = 0.95
epsilon = 1e-08
decay_rate = 0.1
inner_rate = 1.0
outer_rate = 0.7
outer_momentum = 0.9

MESH = pl.DeviceIdType.MESH
F32 = jnp.float32
BF16 = jnp.bfloat16

ORDER = (2, 1, 3, 0)
FAR_FIRST = (4, 3, 5, 2, 6, 1, 7)


def kernel(
    tok_hbm, cot_hbm, par_hbm, first_hbm, second_hbm, anchor_hbm, feed_hbm, mom_hbm, sel_hbm, cnt_hbm,
    key_hbm, anchor_out, feed_out, mom_out,
    tok, cot, cot_t, wts, first, second, anchor, feed, mom, sel, cnt,
    part, sib_in, msg, fin, mark, outg, ybuf, zsrc, zbuf, avg,
    acc, key_v, anchor_v, feed_v, mom_v,
    load_sem, store_sem,
    sib_s, sib_r, x_s, x_r, ag_s, ag_r, rel_s, rel_r,
    y_s, y_r, z_s, z_r, gz_s, gz_r, gy_s, gy_r,
):
    rep = lax.axis_index("rep")
    fs = lax.axis_index("fsdp")
    core = lax.rem(fs, 2)
    x = fs // 2
    y = lax.rem(rep, NY)
    z = rep // NY

    def on_x(k):
        return (rep, lax.rem(x + k, NX) * 2 + core)

    def on_y(k):
        return (z * NY + lax.rem(y + k, NY), fs)

    def on_z(k):
        return (lax.rem(z + k, NZ) * NY + y, fs)

    sib = (rep, x * 2 + 1 - core)

    def remote(src, dst, send, recv, dev):
        return pltpu.make_async_remote_copy(
            src_ref=src, dst_ref=dst, send_sem=send, recv_sem=recv, device_id=dev, device_id_type=MESH
        )

    loads = []

    def load(src, dst):
        c = pltpu.make_async_copy(src, dst, load_sem.at[len(loads)])
        loads.append(c)
        c.start()
        return c

    def load_tok(i):
        chip = lax.rem(x + ORDER[i // 2], NX)
        shard = chip * 2 + (1 - core if i % 2 == 0 else core)
        return load(tok_hbm.at[:, pl.ds(pl.multiple_of(shard * ROWS, ROWS), ROWS)], tok.at[i])

    l_cot = load(cot_hbm, cot)
    l_tok = [load_tok(0), load_tok(1)]

    barrier = pltpu.get_barrier_semaphore()
    peers = [on_z(k) for k in FAR_FIRST] + [on_y(k) for k in range(1, NY)] + [on_x(1), on_x(3), sib]
    for dev in peers:
        pl.semaphore_signal(barrier, inc=1, device_id=dev, device_id_type=MESH)

    l_w = load(par_hbm.at[0], wts.at[7])
    l_tok += [load_tok(i) for i in range(2, 8)]
    l_sel = load(sel_hbm, sel)
    l_cnt = load(cnt_hbm, cnt)
    l_state = [
        load(first_hbm.at[0], first),
        load(second_hbm.at[0], second),
        load(anchor_hbm, anchor),
        load(feed_hbm.at[0], feed),
        load(mom_hbm, mom),
    ]
    l_cot.wait()
    cot_t[...] = jnp.transpose(cot[...], (1, 0))

    ags = []

    def ag(src_slot, dst_slot, rows, size, k):
        n = len(ags)
        c = remote(
            wts.at[src_slot, pl.ds(rows, size)], wts.at[dst_slot, pl.ds(rows, size)], ag_s.at[n], ag_r.at[n], on_x(k)
        )
        c.start()
        ags.append(c)
        return c

    def product(i):
        l_tok[i].wait()
        p = jnp.dot(cot_t[...], tok[i], preferred_element_type=F32)
        p = (p * (1.0 / math.sqrt(D))).astype(BF16)
        for h in range(COLS // PW):
            part[h, i] = p[h * PW : (h + 1) * PW, :]

    sibs = [[], []]

    def exchange(h, i):
        c = remote(part.at[h, 2 * i], sib_in.at[h, i], sib_s.at[h, i], sib_r.at[h, i], sib)
        c.start()
        sibs[h].append(c)

    def x_send(h, n, src, dst, k):
        c = remote(src, dst, x_s.at[h, n], x_r.at[h, n], on_x(k))
        c.start()
        return c

    def pair_sum(h, i, rows):
        s = slice(h % 2 * W + rows, h % 2 * W + rows + HALF)
        return part[h // 2, 2 * i + 1, s, :].astype(F32) + sib_in[h // 2, i, s, :].astype(F32)

    A, B = 0, HALF

    xs = [[] for _ in range(NP)]

    def x_first(h):
        msg[h, 0] = pair_sum(h, 0, A).astype(BF16)
        xs[h].append(x_send(h, 0, msg.at[h, 0], fin.at[h, 0, pl.ds(A, HALF)], 1))
        msg[h, 1] = pair_sum(h, 0, B).astype(BF16)
        xs[h].append(x_send(h, 1, msg.at[h, 1], fin.at[h, 0, pl.ds(B, HALF)], 3))

    def x_plus(h):
        msg[h, 2] = pair_sum(h, 1, B).astype(BF16)
        xs[h].append(x_send(h, 2, msg.at[h, 2], fin.at[h, 1, pl.ds(B, HALF)], 1))

    def x_minus(h):
        msg[h, 3] = pair_sum(h, 2, A).astype(BF16)
        xs[h].append(x_send(h, 3, msg.at[h, 3], fin.at[h, 2, pl.ds(A, HALF)], 3))

    def x_second(h):
        xs[h][0].wait_recv()
        msg[h, 4] = (pair_sum(h, 1, A) + fin[h, 0, A : A + HALF, :].astype(F32)).astype(BF16)
        xs[h].append(x_send(h, 4, msg.at[h, 4], fin.at[h, 1, pl.ds(A, HALF)], 1))
        xs[h][1].wait_recv()
        msg[h, 5] = (pair_sum(h, 2, B) + fin[h, 0, B : B + HALF, :].astype(F32)).astype(BF16)
        xs[h].append(x_send(h, 5, msg.at[h, 5], fin.at[h, 2, pl.ds(B, HALF)], 3))

    def marks():
        l_sel.wait()
        l_cnt.wait()
        place = lax.broadcasted_iota(jnp.int32, (1, KSEL), 1)
        names = jnp.where(place < cnt[...], sel[...], -1)
        ones = jnp.ones((KSEL, W), BF16)
        for b in range(COLS // BLK):
            for r in range(0, ROWS, 128):
                block = (lax.broadcasted_iota(jnp.int32, (128, KSEL), 0) + r) * (COLS // BLK) + b
                hit = jnp.where(block == names, 1.0, 0.0).astype(BF16)
                mark[b, r : r + 128, :] = jnp.dot(hit, ones, preferred_element_type=F32)

    def store(src, dst):
        c = pltpu.make_async_copy(src, dst, store_sem.at[len(stores)])
        stores.append(c)
        c.start()

    stores = []

    def adam(h):
        for n in (2, 3, 4, 5):
            xs[h][n].wait_recv()
        cols = slice(h * W, (h + 1) * W)
        half = slice(h % 2 * W, h % 2 * W + W)
        copies = []
        for k in (2, 1, 3, 0):
            first_row = pl.multiple_of(lax.rem(y + k, NY) * YR, YR)
            block = pl.ds(first_row, YR)
            total = (
                part[h // 2, 7, half, block].astype(F32) + sib_in[h // 2, 3, half, block].astype(F32)
                + fin[h, 1, :, block].astype(F32) + fin[h, 2, :, block].astype(F32)
            )
            gradient = jnp.transpose(total, (1, 0))
            for r in range(0, YR, 32):
                s = pl.ds(pl.multiple_of(first_row + r, 32), 32)
                g = gradient[r : r + 32, :]
                first_new = beta_first * first[s, cols] + (1.0 - beta_first) * g
                second_new = beta_second * second[s, cols] + (1.0 - beta_second) * g * g
                master = wts[7, s, cols].astype(F32)
                stepped = master - inner_rate * (
                    first_new / (jnp.sqrt(second_new) + epsilon) + decay_rate * master
                )
                combined = feed[s, cols] + (anchor[s, cols] - stepped)
                marked = mark[h * W // BLK, s, :] > 0.5
                feed_v[h, s, :] = jnp.where(marked, 0.0, combined)
                outg[h, s, :] = jnp.where(marked, combined, 0.0).astype(BF16)
            if k > 0:
                c = remote(outg.at[h, block], ybuf.at[h, k - 1], y_s.at[h, k - 1], y_r.at[h, k - 1], on_y(k))
                c.start()
                copies.append(c)
        store(feed_v.at[h], feed_out.at[0, :, pl.ds(h * W, W)])
        return copies

    def sync_z(h, c):
        for one in c:
            one.wait_recv()
        total = outg[h, pl.ds(pl.multiple_of(y * YR, YR), YR), :].astype(F32)
        for k in range(NY - 1):
            total = total + ybuf[h, k].astype(F32)
        zsrc[h] = total.astype(BF16)
        copies = []
        for k in FAR_FIRST:
            to = lax.rem(z + k, NZ)
            c = remote(
                zsrc.at[h, pl.ds(pl.multiple_of(to * ZR, ZR), ZR)], zbuf.at[h, k - 1],
                z_s.at[h, k - 1], z_r.at[h, k - 1], on_z(k),
            )
            c.start()
            copies.append(c)
        return copies

    def gather_z(h, c):
        for one in c:
            one.wait_recv()
        total = zsrc[h, pl.ds(pl.multiple_of(z * ZR, ZR), ZR), :].astype(F32)
        for k in range(NZ - 1):
            total = total + zbuf[h, k].astype(F32)
        mine = pl.ds(pl.multiple_of(y * YR + z * ZR, ZR), ZR)
        avg[h, mine, :] = (total * (1.0 / (NY * NZ))).astype(BF16)
        copies = []
        for k in FAR_FIRST:
            c = remote(avg.at[h, mine], avg.at[h, mine], gz_s.at[h, k - 1], gz_r.at[h, k - 1], on_z(k))
            c.start()
            copies.append(c)
        return copies

    def gather_y(h, c):
        for one in c:
            one.wait_recv()
        mine = pl.ds(pl.multiple_of(y * YR, YR), YR)
        copies = []
        for k in range(1, NY):
            c = remote(avg.at[h, mine], avg.at[h, mine], gy_s.at[h, k - 1], gy_r.at[h, k - 1], on_y(k))
            c.start()
            copies.append(c)
        return copies

    def outer(h, c):
        for one in c:
            one.wait_recv()
        cols = slice(h * W, (h + 1) * W)

        def body(n, _):
            s = pl.ds(pl.multiple_of(n * 32, 32), 32)
            average = avg[h, s, :].astype(F32)
            momentum_new = outer_momentum * mom[s, cols] + average
            mom_v[h, s, :] = momentum_new
            anchor_v[h, s, :] = anchor[s, cols] - outer_rate * (average + outer_momentum * momentum_new)
            return 0

        lax.fori_loop(0, ROWS // 32, body, 0)
        store(mom_v.at[h], mom_out.at[:, pl.ds(h * W, W)])
        store(anchor_v.at[h], anchor_out.at[:, pl.ds(h * W, W)])

    def key_block(slots, begin=False):
        p = None if begin else acc[...]
        for slot in slots:
            q = jnp.dot(tok[slot], wts[slot], preferred_element_type=F32)
            p = q if p is None else p + q
        acc[...] = p

    rel = []

    def relay(slot, rows, size):
        n = len(rel)
        c = remote(
            wts.at[slot, pl.ds(rows, size)], wts.at[slot - 1, pl.ds(rows, size)], rel_s.at[n], rel_r.at[n], sib
        )
        c.start()
        rel.append(c)

    ys, zs, gzs, gys = [None] * NP, [None] * NP, [None] * NP, [None] * NP
    product(0)
    pl.semaphore_wait(barrier, len(peers))
    exchange(0, 0)
    l_w.wait()
    plus = [ag(7, 5, 0, 64, 1)]
    minus = [ag(7, 3, 256, 64, 3)]
    product(1)
    sibs[0][0].wait_recv()
    x_first(0)
    x_first(1)
    product(2)
    exchange(0, 1)
    exchange(1, 0)
    product(3)
    product(4)
    exchange(0, 2)
    exchange(1, 1)
    exchange(1, 2)
    sibs[1][0].wait_recv()
    x_first(2)
    x_first(3)
    sibs[0][1].wait_recv()
    x_plus(0)
    product(5)
    sibs[0][2].wait_recv()
    x_minus(0)
    x_second(0)
    x_plus(1)
    x_minus(1)
    product(6)
    exchange(0, 3)
    exchange(1, 3)
    x_second(1)
    sibs[1][1].wait_recv()
    x_plus(2)
    sibs[1][2].wait_recv()
    x_minus(2)
    product(7)
    x_second(2)
    x_plus(3)
    x_minus(3)
    marks()
    x_second(3)
    relay(7, 0, ROWS)
    plus += [ag(7, 5, 64, 192, 1)]
    minus += [ag(7, 3, 320, 192, 3)]
    plus[0].wait_recv()
    minus[0].wait_recv()
    plus += [ag(5, 1, 0, 64, 1), ag(7, 5, 256, 256, 1)]
    minus += [ag(3, 1, 256, 64, 3), ag(7, 3, 0, 256, 3)]
    relay(5, 0, 64)
    relay(3, 256, 64)
    for one in l_state:
        one.wait()
    sibs[0][3].wait_recv()
    ys[0] = adam(0)
    rel[0].wait_recv()
    key_block((7, 6), begin=True)
    ys[1] = adam(1)
    zs[0] = sync_z(0, ys[0])
    sibs[1][3].wait_recv()
    ys[2] = adam(2)
    zs[1] = sync_z(1, ys[1])
    ys[3] = adam(3)

    zs[2] = sync_z(2, ys[2])
    zs[3] = sync_z(3, ys[3])
    plus[1].wait_recv()
    plus.append(ag(5, 1, 64, 192, 1))
    minus[1].wait_recv()
    minus.append(ag(3, 1, 320, 192, 3))
    relay(5, 64, 192)
    relay(3, 320, 192)
    gzs[0] = gather_z(0, zs[0])
    gzs[1] = gather_z(1, zs[1])
    plus[2].wait_recv()
    relay(1, 0, 64)
    minus[2].wait_recv()
    relay(1, 256, 64)
    gzs[2] = gather_z(2, zs[2])
    gzs[3] = gather_z(3, zs[3])
    for h in range(NP - 1):
        gys[h] = gather_y(h, gzs[h])
    plus[3].wait_recv()
    relay(5, 256, 256)
    minus[3].wait_recv()
    relay(3, 0, 256)
    key_block((5, 3))
    gys[3] = gather_y(3, gzs[3])
    outer(0, gys[0])
    plus[4].wait_recv()
    relay(1, 64, 192)
    minus[4].wait_recv()
    relay(1, 320, 192)
    key_block((1,))
    outer(1, gys[1])
    outer(2, gys[2])
    for one in rel[1:]:
        one.wait_recv()
    key_block((4, 2, 0))
    key_v[...] = (acc[...] * (1.0 / math.sqrt(D))).astype(BF16)
    store(key_v, key_hbm)
    outer(3, gys[3])

    for group in sibs + xs + ys + zs + gzs + gys + [ags, rel]:
        for one in group:
            one.wait_send()
    for one in stores:
        one.wait()


def flush(*refs):
    sem = refs[-1]
    copies = [pltpu.make_async_copy(refs[n], refs[4 + n], sem.at[n]) for n in range(4)]
    for one in copies:
        one.start()
    for one in copies:
        one.wait()


def shards(
    tokens,
    cotangent,
    inner_params,
    first_moment,
    second_moment,
    anchor,
    feedback,
    momentum,
    sel_blocks,
    sel_count,
):
    dma = pltpu.SemaphoreType.DMA
    any_space = pl.BlockSpec(memory_space=pl.ANY)
    hbm = pl.BlockSpec(memory_space=pltpu.HBM)
    outs = (
            jax.ShapeDtypeStruct((TOK, COLS), BF16),
            jax.ShapeDtypeStruct((ROWS, COLS), F32),
            jax.ShapeDtypeStruct((1, ROWS, COLS), F32),
            jax.ShapeDtypeStruct((ROWS, COLS), F32),
        )
    done = pl.pallas_call(
        kernel,
        out_shape=outs,
        in_specs=[hbm] * 10,
        out_specs=(any_space,) * 4,
        scratch_shapes=[
            pltpu.VMEM((8, TOK, ROWS), BF16),
            pltpu.VMEM((TOK, COLS), BF16),
            pltpu.VMEM((COLS, TOK), BF16),
            pltpu.VMEM((8, ROWS, COLS), BF16),
            pltpu.VMEM((ROWS, COLS), F32),
            pltpu.VMEM((ROWS, COLS), F32),
            pltpu.VMEM((ROWS, COLS), F32),
            pltpu.VMEM((ROWS, COLS), F32),
            pltpu.VMEM((ROWS, COLS), F32),
            pltpu.VMEM((1, KSEL), jnp.int32),
            pltpu.VMEM((1, 1), jnp.int32),
            pltpu.VMEM((COLS // PW, 8, PW, ROWS), BF16),
            pltpu.VMEM((COLS // PW, 4, PW, ROWS), BF16),
            pltpu.VMEM((NP, 6, HALF, ROWS), BF16),
            pltpu.VMEM((NP, 3, W, ROWS), BF16),
            pltpu.VMEM((COLS // BLK, ROWS, W), F32),
            pltpu.VMEM((NP, ROWS, W), BF16),
            pltpu.VMEM((NP, NY - 1, YR, W), BF16),
            pltpu.VMEM((NP, YR, W), BF16),
            pltpu.VMEM((NP, NZ - 1, ZR, W), BF16),
            pltpu.VMEM((NP, ROWS, W), BF16),
            pltpu.VMEM((TOK, COLS), F32),
            pltpu.VMEM((TOK, COLS), BF16),
            pltpu.VMEM((NP, ROWS, W), F32),
            pltpu.VMEM((NP, ROWS, W), F32),
            pltpu.VMEM((NP, ROWS, W), F32),
            dma((17,)),
            dma((3 * NP + 1,)),
            dma((COLS // PW, 4)),
            dma((COLS // PW, 4)),
            dma((NP, 6)),
            dma((NP, 6)),
            dma((10,)),
            dma((10,)),
            dma((11,)),
            dma((11,)),
            dma((NP, NY - 1)),
            dma((NP, NY - 1)),
            dma((NP, NZ - 1)),
            dma((NP, NZ - 1)),
            dma((NP, NZ - 1)),
            dma((NP, NZ - 1)),
            dma((NP, NY - 1)),
            dma((NP, NY - 1)),
        ],
        compiler_params=pltpu.CompilerParams(
            collective_id=0, has_side_effects=True, vmem_limit_bytes=40 * 1024 * 1024
        ),
        cost_estimate=pl.CostEstimate(flops=4 * TOK * D * COLS, bytes_accessed=14 * 2**20, transcendentals=0),
    )(
        *(
            pltpu.with_memory_space_constraint(a, pltpu.HBM)
            for a in (
                tokens, cotangent, inner_params, first_moment, second_moment, anchor, feedback, momentum,
                sel_blocks.reshape(1, KSEL),
            )
        ),
        sel_count.reshape(1, 1),
    )
    return pl.pallas_call(
        flush,
        out_shape=outs,
        in_specs=[any_space] * 4,
        out_specs=(any_space,) * 4,
        scratch_shapes=[dma((4,))],
        compiler_params=pltpu.CompilerParams(has_side_effects=True, vmem_limit_bytes=4 * 1024 * 1024),
    )(*done)


def solution(mesh):
    placed = (
        P(("rep", "fsdp"), None),
        P(("rep", "fsdp"), None),
        P("rep", "fsdp", None),
        P("rep", "fsdp", None),
        P("rep", "fsdp", None),
        P("fsdp", None),
        P("rep", "fsdp", None),
        P("fsdp", None),
        P("rep", "fsdp", None),
        P("rep", "fsdp"),
    )
    return jax.shard_map(
        shards,
        mesh=mesh,
        in_specs=placed,
        out_specs=(
            P(("rep", "fsdp"), None),
            P("fsdp", None),
            P("rep", "fsdp", None),
            P("fsdp", None),
        ),
        check_vma=False,
    )
```
